32 devices in a mesh: group: 2 (over y), expert: 4 (over z), dp: 4 (over x, core).
Axes of the slice: x: 2, y: 2, z: 4, core: 2. Of those that a mesh axis runs over, the one named last changes fastest.
Arguments:
- latent_in: bfloat16 [2048, 1024], P(('group', 'expert', 'dp')), parts along dimension 0, may hold values from -6 to 6
- routes: int32 [2048, 8], P(('group', 'expert', 'dp')), parts along dimension 0, may hold values from 0 to 15, all different within a row; in each aligned block of 64 rows (0 to 63, 64 to 127, ...) at most 36 rows name the same one
- gates: float32 [2048, 8], P(('group', 'expert', 'dp')), parts along dimension 0, may hold values from 0.02 to 0.3
- up_weight: bfloat16 [16, 1024, 1024], P('expert', 'dp'), may hold values from -0.1875 to 0.1875
- down_weight: bfloat16 [16, 1024, 1024], P('expert', 'dp'), may hold values from -0.1875 to 0.1875
- out_grad: bfloat16 [2048, 1024], P(('group', 'expert', 'dp')), parts along dimension 0, may hold values from -6 to 6
Outputs:
- latent_out: bfloat16 [2048, 1024], P(('group', 'expert', 'dp')), parts along dimension 0
- grad_in: bfloat16 [2048, 1024], P(('group', 'expert', 'dp')), parts along dimension 0
- gate_grad: float32 [2048, 8], P(('group', 'expert', 'dp')), parts along dimension 0
- grad_up: float32 [32, 1024, 1024], P(('group', 'expert'), 'dp'), parts along dimension 0
- grad_down: float32 [32, 1024, 1024], P(('group', 'expert'), 'dp'), parts along dimension 0
The draws below stay inside these ranges and needn't reach their ends.
There are 2 independent parts, one for each index of `group`. The reference program is written for one: setup_inputs(seed, part) draws one part's arguments, and reference() takes and returns one part's arrays. A program takes and returns all parts, laid end to end along the dimension named above; an argument that names none is the same for every part. Nothing has to cross between parts.
Inputs may be any that keep to these rules, and one draw needn't show every extreme that they name: `routes`: in each aligned block of 64 rows (the rows of one device) no expert is named by more than 36 rows, and in some blocks one is named by exactly 36; the 8 experts of a row differ.
All inputs are finite; a program needn't handle non-finite values.
Results may differ from the reference program's by a relative error of at most 0.015.
Values may be sent and summed in bfloat16 or wider, within the bound.
A program may use at most 128 MiB of HBM per device.

```python
import math
import jax
import jax.numpy as jnp
import numpy as np
from jax import lax

L = 1024
H = 1024
TOP = 8
TOK_DEV = 64
EXPERTS = 16
CAP = 36
TOKENS = 1024
N_EXPERT = 4
N_DP = 4


def shard_levels(key, dims, pieces, low, top_value):
    level = 1.0
    for dim, parts in pieces:
        draws = jax.random.uniform(jax.random.fold_in(jax.random.fold_in(key, 6), dim), (parts,), jnp.float32, low / len(pieces), top_value / len(pieces))
        level = level * jnp.repeat(jnp.exp(draws), dims[dim] // parts).reshape((-1,) + (1,) * (len(dims) - 1 - dim))
    return level


def shared_out(own_key, own, number, rows, amount, top, reach, skew):
    sequence = jax.random.permutation(own_key, amount)
    crowded, ordinary = portions_of(amount, rows * top, reach, skew, True), portions_of(amount, rows * top, reach, skew, False)
    places = jnp.arange(amount)

    def named(lengths, offset_by):
        used = int((lengths > 0).sum())
        fixed = max(1, used // 4)
        moved = fixed + (places - fixed + offset_by * (used - fixed)) % max(1, amount - fixed)
        return jnp.zeros((amount,), jnp.int32).at[sequence[jnp.where(places < fixed, places, moved)]].set(jnp.asarray(lengths, jnp.int32))

    lengths = jnp.where(number % 4 == 0, named(crowded, number // 4), named(ordinary, number - number // 4 - 1))
    mixed = jax.random.permutation(jax.random.fold_in(own, 3), amount)
    donor, taker = mixed[0:amount // 2 * 2:2], mixed[1:amount // 2 * 2:2]
    slack = jnp.minimum(lengths[donor] - 1, reach - lengths[taker]) // 2
    slack = jnp.where((donor == sequence[0]) | (taker == sequence[0]) | (lengths[taker] == 0), 0, jnp.maximum(slack, 0))
    moved = jax.random.randint(jax.random.fold_in(own, 4), (amount // 2,), 0, 1 << 20) % (slack + 1)
    lengths = lengths.at[donor].add(-moved).at[taker].add(moved)
    members = jnp.searchsorted(jnp.cumsum(lengths), jnp.arange(rows * top), side="right").astype(jnp.int32)
    listing = members.reshape(top, rows).T
    listing = listing[jax.random.permutation(jax.random.fold_in(own, 1), rows)]
    offset_by = jax.random.randint(jax.random.fold_in(own, 2), (rows, 1), 0, top)
    return jnp.take_along_axis(listing, (jnp.arange(top)[None, :] + offset_by) % top, axis=1)


def portions_of(amount, total, reach, slope, full):
    loads = [(1 << 20) // math.isqrt(grade ** slope) + 1 for grade in range(1, amount + 1)]
    largest = reach if full else min(reach, max(-(-total // amount), total * loads[0] // sum(loads)))
    least = 1 if total - largest >= amount - 1 else 0
    counts, surplus = [largest] + [least] * (amount - 1), total - largest - least * (amount - 1)
    while surplus > 0:
        free = [i for i in range(1, amount) if counts[i] < largest] or [i for i in range(1, amount) if counts[i] < reach]
        whole, remaining = sum([loads[i] for i in free]), surplus
        for i in free:
            addition = min(reach - counts[i], max(1, remaining * loads[i] // whole), surplus)
            counts[i] = counts[i] + addition
            surplus = surplus - addition
    return np.array(counts)


def scatter_about(own_key, dims, width, most, shards=(), kind=jnp.bfloat16):
    loudness = shard_levels(own_key, dims, shards, -0.22, 0.18) if shards else 1.0
    entries = jax.random.normal(own_key, dims, jnp.float32) * width * loudness
    return jnp.minimum(jnp.maximum(entries, -most), most).astype(kind)


def setup_inputs(seed: int = 0, part: int = 0) -> dict:
    seeds = jax.random.split(jax.random.key(seed), 7)
    own_keys = jax.random.split(jax.random.fold_in(seeds[6], part), 7)
    latent_in = scatter_about(own_keys[0], (TOKENS, L), 1.0, 6.0, ((0, 16),))
    routes_keys = jax.random.split(jax.random.fold_in(own_keys[1], 1), TOKENS // TOK_DEV)
    routes_turns = jax.random.permutation(jax.random.fold_in(own_keys[1], 3), TOKENS // TOK_DEV)
    routes = jax.vmap(lambda own, number: shared_out(jax.random.fold_in(own_keys[1], 2), own, number, TOK_DEV, EXPERTS, TOP, CAP, 2))(routes_keys, routes_turns).reshape((TOKENS, TOP))
    gates = jnp.clip(0.02 + 0.28 * jax.random.uniform(own_keys[2], (TOKENS, TOP), jnp.float32) ** shard_levels(own_keys[2], (TOKENS, TOP), ((0, 16),), -0.2, 0.2), 0.02, 0.3)
    up_weight = scatter_about(seeds[3], (EXPERTS, L, H), L ** -0.5, 0.1875, ((0, 4), (1, 4)))
    down_weight = scatter_about(seeds[4], (EXPERTS, H, L), H ** -0.5, 0.1875, ((0, 4), (1, 4)))
    out_grad = scatter_about(own_keys[5], (TOKENS, L), 1.0, 6.0, ((0, 16),))
    return dict(latent_in=latent_in, routes=routes, gates=gates, up_weight=up_weight, down_weight=down_weight, out_grad=out_grad)


def rounded(values):
    return lax.optimization_barrier(values.astype(jnp.bfloat16)).astype(jnp.float32)


def slot_table(routes, blocks):
    pair_routes = routes.reshape(blocks, TOK_DEV * TOP)
    onehot = (pair_routes[:, :, None] == jnp.arange(EXPERTS, dtype=jnp.int32)[None, None, :]).astype(jnp.int32)
    earlier = jnp.cumsum(onehot, axis=1) - onehot
    slot_ids = jnp.sum(earlier * onehot, axis=2).astype(jnp.int32)
    pair_ids = jnp.broadcast_to(jnp.arange(TOK_DEV * TOP, dtype=jnp.int32)[None, :], pair_routes.shape)
    block_ids = jnp.broadcast_to(jnp.arange(blocks, dtype=jnp.int32)[:, None], pair_routes.shape)
    filled = jnp.full((blocks, EXPERTS, CAP), TOK_DEV * TOP, dtype=jnp.int32)
    return filled.at[block_ids, pair_routes, slot_ids].set(pair_ids)


def reference(latent_in, routes, gates, up_weight, down_weight, out_grad):
    blocks = latent_in.shape[0] // TOK_DEV
    latent = latent_in.shape[1]
    pair_total = TOK_DEV * TOP
    filled = slot_table(routes, blocks)
    zero_rows = jnp.zeros((blocks, 1, latent), jnp.bfloat16)
    rows_in = jnp.concatenate([latent_in.reshape(blocks, TOK_DEV, latent), zero_rows], axis=1)
    rows_grad = jnp.concatenate([out_grad.reshape(blocks, TOK_DEV, latent), zero_rows], axis=1)
    gate_rows = jnp.concatenate([gates.reshape(blocks, pair_total), jnp.zeros((blocks, 1), jnp.float32)], axis=1)
    block_ids = jnp.arange(blocks, dtype=jnp.int32)[:, None]

    def per_expert(carry, inputs):
        out_acc, grad_acc, gate_acc = carry
        pair_ids, up_mat, down_mat = inputs
        token_ids = (pair_ids // TOP).astype(jnp.int32)
        picked_in = jnp.take_along_axis(rows_in, token_ids[:, :, None], axis=1).astype(jnp.float32)
        picked_dy = jnp.take_along_axis(rows_grad, token_ids[:, :, None], axis=1).astype(jnp.float32)
        slot_gate = jnp.take_along_axis(gate_rows, pair_ids, axis=1)
        up_wide = up_mat.astype(jnp.float32)
        down_wide = down_mat.astype(jnp.float32)
        pre_act = jnp.einsum("bcl,lh->bch", picked_in, up_wide)
        active = jnp.maximum(pre_act, 0.0)
        hidden = (active * active).astype(jnp.bfloat16).astype(jnp.float32)
        result = jnp.einsum("bch,hl->bcl", hidden, down_wide).astype(jnp.bfloat16).astype(jnp.float32)
        out_acc = out_acc.at[block_ids, token_ids].add(slot_gate[:, :, None] * result)
        gate_acc = gate_acc.at[block_ids, pair_ids].add(jnp.sum(picked_dy * result, axis=2))
        out_part = (slot_gate[:, :, None] * picked_dy).astype(jnp.bfloat16).astype(jnp.float32)
        hidden_grad = jnp.einsum("bcl,hl->bch", out_part, down_wide)
        pre_grad = (hidden_grad * 2.0 * active).astype(jnp.bfloat16).astype(jnp.float32)
        row_grad = jnp.einsum("bch,lh->bcl", pre_grad, up_wide).astype(jnp.bfloat16).astype(jnp.float32)
        grad_acc = grad_acc.at[block_ids, token_ids].add(row_grad)
        up_part = jnp.einsum("sdcl,sdch->dlh", picked_in.reshape(N_EXPERT, N_DP, CAP, latent), pre_grad.reshape(N_EXPERT, N_DP, CAP, -1))
        down_part = jnp.einsum("sdch,sdcl->dhl", hidden.reshape(N_EXPERT, N_DP, CAP, -1), out_part.reshape(N_EXPERT, N_DP, CAP, latent))
        up_sum = jnp.sum(rounded(up_part), axis=0)
        down_sum = jnp.sum(rounded(down_part), axis=0)
        return (out_acc, grad_acc, gate_acc), (up_sum, down_sum)

    start = (jnp.zeros((blocks, TOK_DEV + 1, latent), jnp.float32), jnp.zeros((blocks, TOK_DEV + 1, latent), jnp.float32), jnp.zeros((blocks, pair_total + 1), jnp.float32))
    carry, stacked = lax.scan(per_expert, start, (jnp.transpose(filled, (1, 0, 2)), up_weight, down_weight))
    out_acc, grad_acc, gate_acc = carry
    latent_out = out_acc[:, :TOK_DEV].reshape(-1, latent).astype(jnp.bfloat16)
    grad_in = grad_acc[:, :TOK_DEV].reshape(-1, latent).astype(jnp.bfloat16)
    gate_grad = gate_acc[:, :pair_total].reshape(-1, TOP)
    return (latent_out, grad_in, gate_grad, stacked[0], stacked[1])
```

```python
import jax
import jax.numpy as jnp
from jax import lax
from jax.sharding import PartitionSpec as P

BOTH = ("expert", "dp")


def by_tokens(latent_in, routes, gates, up_weight, down_weight, out_grad):
    owners, parts = lax.axis_size("expert"), lax.axis_size("dp")
    experts, depth, hid = up_weight.shape
    latent = latent_in.shape[1]
    total = experts * owners
    width = hid // parts
    ids = jnp.arange(total, dtype=jnp.int32)
    chosen = routes[:, :, None] == ids[None, None, :]
    table = jnp.sum(jnp.where(chosen, gates[:, :, None], 0.0), axis=1)

    up = lax.all_to_all(up_weight, "dp", split_axis=2, concat_axis=1, tiled=True)
    rows = lax.all_gather(latent_in, BOTH, axis=0, tiled=True)
    dy = lax.all_gather(out_grad, BOTH, axis=0, tiled=True)
    table_all = lax.all_gather(table, BOTH, axis=0, tiled=True)
    first = lax.axis_index("expert") * experts
    weight = lax.dynamic_slice_in_dim(table_all, first, experts, axis=1)
    weight = jnp.transpose(weight)[:, :, None]

    pre = jnp.einsum("tl,elh->eth", rows, up, preferred_element_type=jnp.float32)
    back = jnp.einsum("tl,ehl->eth", dy, down_weight, preferred_element_type=jnp.float32)
    active = jnp.where(weight > 0.0, jnp.maximum(pre, 0.0), 0.0)
    hidden = active * active
    gate_part = jnp.sum(hidden * back, axis=2)
    gated = (weight * hidden).astype(jnp.bfloat16)
    pre_grad = (weight * back * 2.0 * active).astype(jnp.bfloat16)
    out = jnp.einsum("eth,ehl->tl", gated, down_weight, preferred_element_type=jnp.float32)
    gin = jnp.einsum("eth,elh->tl", pre_grad, up, preferred_element_type=jnp.float32)
    both = jnp.stack([out, gin], axis=1).astype(jnp.bfloat16)
    both = lax.psum_scatter(both, BOTH, scatter_dimension=0, tiled=True)
    gsum = jnp.zeros((rows.shape[0], total), jnp.float32)
    gsum = lax.dynamic_update_slice_in_dim(gsum, jnp.transpose(gate_part), first, axis=1)
    gsum = lax.psum_scatter(gsum, BOTH, scatter_dimension=0, tiled=True)
    gate_grad = jnp.sum(jnp.where(chosen, gsum[:, None, :], 0.0), axis=2)
    grad_up = jnp.einsum("tl,eth->elh", rows, pre_grad, preferred_element_type=jnp.float32)
    grad_up = lax.all_to_all(
        grad_up.astype(jnp.bfloat16), "dp", split_axis=1, concat_axis=2, tiled=True
    ).astype(jnp.float32)
    grad_down = jnp.einsum("eth,tl->ehl", gated, dy, preferred_element_type=jnp.float32)
    return (both[:, 0], both[:, 1], gate_grad, grad_up, grad_down)


def slot_places(routes, expert_total, capacity):
    flat_ids = routes.reshape(-1)
    pair_count = flat_ids.shape[0]
    onehot = (flat_ids[:, None] == jnp.arange(expert_total, dtype=jnp.int32)[None, :]).astype(
        jnp.int32
    )
    earlier = jnp.cumsum(onehot, axis=0) - onehot
    slot_ids = jnp.sum(earlier * onehot, axis=1)
    places = flat_ids * capacity + slot_ids
    empty = jnp.full((expert_total * capacity,), pair_count, jnp.int32)
    pair_of = empty.at[places].set(jnp.arange(pair_count, dtype=jnp.int32))
    return (places, pair_of)


def by_rows(latent_in, routes, gates, up_weight, down_weight, out_grad):
    owner_count = lax.axis_size("expert")
    local_experts = up_weight.shape[0]
    expert_total = local_experts * owner_count
    token_rows, route_count = routes.shape
    latent = latent_in.shape[1]
    capacity = 9 * token_rows * route_count // (8 * expert_total)
    places, pair_of = slot_places(routes, expert_total, capacity)
    token_of = pair_of // route_count
    zero_row = jnp.zeros((1, latent), jnp.bfloat16)
    padded_in = jnp.concatenate([latent_in, zero_row], axis=0)
    padded_grad = jnp.concatenate([out_grad, zero_row], axis=0)
    padded_gates = jnp.concatenate([gates.reshape(-1), jnp.zeros((1,), jnp.float32)])
    slot_gates = padded_gates[pair_of]
    send_shape = (owner_count, local_experts * capacity, latent)
    block_shape = (owner_count, local_experts, capacity, latent)
    send_rows = padded_in[token_of].reshape(send_shape)
    send_grad = (
        (slot_gates[:, None] * padded_grad[token_of].astype(jnp.float32))
        .astype(jnp.bfloat16)
        .reshape(send_shape)
    )
    up_full, down_full = (
        lax.all_gather(up_weight, "dp", axis=1, tiled=True),
        lax.all_gather(down_weight, "dp", axis=1, tiled=True),
    )
    arrived = lax.all_to_all(send_rows, "expert", split_axis=0, concat_axis=0, tiled=True)
    forward_rows_four = arrived.reshape(block_shape)
    pre_act = jnp.einsum(
        "secl,elh->sech", forward_rows_four, up_full, preferred_element_type=jnp.float32
    )
    active = jnp.maximum(pre_act, 0.0)
    forward_hidden = (active * active).astype(jnp.bfloat16)
    result = jnp.einsum(
        "sech,ehl->secl", forward_hidden, down_full, preferred_element_type=jnp.float32
    ).astype(jnp.bfloat16)
    rows_four, active, hidden, result = (
        forward_rows_four,
        active,
        forward_hidden,
        result.reshape(send_shape),
    )
    returned = lax.all_to_all(result, "expert", split_axis=0, concat_axis=0, tiled=True)
    arrived_grad = lax.all_to_all(send_grad, "expert", split_axis=0, concat_axis=0, tiled=True)
    backward_grad_four = arrived_grad.reshape(block_shape)
    hidden_grad = jnp.einsum(
        "secl,ehl->sech", backward_grad_four, down_full, preferred_element_type=jnp.float32
    )
    backward_pre_grad = (hidden_grad * 2.0 * active).astype(jnp.bfloat16)
    row_grad = jnp.einsum(
        "sech,elh->secl", backward_pre_grad, up_full, preferred_element_type=jnp.float32
    ).astype(jnp.bfloat16)
    grad_four, pre_grad, row_grad = (
        backward_grad_four,
        backward_pre_grad,
        row_grad.reshape(send_shape),
    )
    returned_grad = lax.all_to_all(row_grad, "expert", split_axis=0, concat_axis=0, tiled=True)
    picked = (
        returned.reshape(expert_total * capacity, latent)[places]
        .reshape(token_rows, route_count, latent)
        .astype(jnp.float32)
    )
    latent_out = jnp.sum(gates[:, :, None] * picked, axis=1).astype(jnp.bfloat16)
    gate_grad = jnp.sum(out_grad.astype(jnp.float32)[:, None, :] * picked, axis=2)
    picked_grad = (
        returned_grad.reshape(expert_total * capacity, latent)[places]
        .reshape(token_rows, route_count, latent)
        .astype(jnp.float32)
    )
    grad_in = jnp.sum(picked_grad, axis=1).astype(jnp.bfloat16)
    up_sum = lax.psum_scatter(
        jnp.einsum(
            "secl,sech->leh", rows_four, pre_grad, preferred_element_type=jnp.float32
        ).astype(jnp.bfloat16),
        "dp",
        scatter_dimension=0,
        tiled=True,
    ).astype(jnp.float32)
    down_sum = lax.psum_scatter(
        jnp.einsum("sech,secl->hel", hidden, grad_four, preferred_element_type=jnp.float32).astype(
            jnp.bfloat16
        ),
        "dp",
        scatter_dimension=0,
        tiled=True,
    ).astype(jnp.float32)
    grad_up = jnp.transpose(up_sum, (1, 0, 2))
    grad_down = jnp.transpose(down_sum, (1, 0, 2))
    return (latent_out, grad_in, gate_grad, grad_up, grad_down)


def local(*args):
    token_bytes = args[0].size * 2 * lax.axis_size("expert") * lax.axis_size("dp")
    if token_bytes <= 4 << 20:
        return by_tokens(*args)
    return by_rows(*args)


def solution(mesh):
    tokens = P(("group", "expert", "dp"), None)
    weights = P("expert", "dp", None)
    grads = P(("group", "expert"), "dp", None)
    return jax.shard_map(
        local,
        mesh=mesh,
        in_specs=(tokens, tokens, tokens, weights, weights, tokens),
        out_specs=(tokens, tokens, tokens, grads, grads),
        check_vma=False,
    )
```

```python
import functools

import jax
import jax.numpy as jnp
from jax import lax
from jax.experimental import pallas as pl
from jax.experimental.pallas import tpu as pltpu
from jax.sharding import PartitionSpec as P

BF16, F32 = jnp.bfloat16, jnp.float32
LANES = 128


def dot(a, b, left=1, right=0):
    return lax.dot_general(a, b, (((left,), (right,)), ((), ())), preferred_element_type=F32)


def kernel(
    owners, lat_ref, routes_ref, gates_ref, up_ref, down_ref, dy_ref,
    out_ref, gin_ref, gate_ref, gup_ref, gdown_ref,
    tok, tab, upt, gated, pgrad, part, gpart, prec, pgrec, xrec, xgrec, tot, gtot, zrec, zgrec,
    gsend, grec,
    z_s, z_r, x_s, x_r, s_s, s_r, u_s, u_r, p_s, p_r, y_s, y_r, w_s, w_r, g_s, g_r,
):
    block = lat_ref.shape[0]
    experts, depth, hid = up_ref.shape
    width = hid // 4
    z, d = lax.axis_index("expert"), lax.axis_index("dp")
    sib, across, diag = d + 1 - 2 * (d % 2), (d + 2) % 4, 3 - d
    mates = (d, sib, across, diag)
    first = z * experts

    def zat(r):
        return (z + r) % owners

    def rows_of(zs):
        return pl.ds(pl.multiple_of(zs * block, block), block)

    def cut(i, size):
        return pl.ds(pl.multiple_of(i * size, size), size)

    def copy(src, dst, send, recv, where):
        return pltpu.make_async_remote_copy(
            src_ref=src, dst_ref=dst, send_sem=send, recv_sem=recv,
            device_id=where, device_id_type=pl.DeviceIdType.MESH,
        )

    sent = []

    def go(c):
        c.start()
        sent.append(c)

    barrier = pltpu.get_barrier_semaphore()
    for m in mates[1:]:
        pl.semaphore_signal(barrier, inc=1, device_id={"dp": m}, device_id_type=pl.DeviceIdType.MESH)
    for r in range(1, owners):
        pl.semaphore_signal(
            barrier, inc=1, device_id={"expert": zat(r)}, device_id_type=pl.DeviceIdType.MESH
        )

    lane = lax.broadcasted_iota(jnp.int32, (block, LANES), 1)
    routes, gates = routes_ref[...], gates_ref[...]
    tops = routes.shape[1]
    table = jnp.zeros((block, LANES), F32)
    for k in range(tops):
        table += jnp.where(lane == routes[:, k : k + 1], gates[:, k : k + 1], 0.0)
    tok[d, 0, rows_of(z), :] = lat_ref[...]
    tok[d, 1, rows_of(z), :] = dy_ref[...]
    tab[d, rows_of(z), :] = table
    pl.semaphore_wait(barrier, 3 + owners - 1)

    def blocks(dd, zs, send, recv, i, where):
        a, b = tok.at[dd, :, rows_of(zs), :], tab.at[dd, rows_of(zs), :]
        return (
            copy(a, a, send.at[0, i], recv.at[0, i], where),
            copy(b, b, send.at[1, i], recv.at[1, i], where),
        )

    def send_blocks(*args):
        for c in blocks(*args):
            go(c)

    def wait_blocks(*args):
        for c in blocks(*args):
            c.wait_recv()

    to_sib, to_x = {"dp": sib}, {"dp": across}
    for r in range(1, owners):
        send_blocks(d, z, z_s, z_r, r - 1, {"expert": zat(owners - r)})
    send_blocks(d, z, x_s, x_r, 0, to_x)
    send_blocks(d, z, s_s, s_r, 0, to_sib)
    for j in (1, 2, 3):
        m = mates[j]
        go(copy(up_ref.at[:, :, cut(m, width)], upt.at[:, cut(d, depth), :],
                u_s.at[j - 1], u_r.at[j - 1], {"dp": m}))
    upt[:, cut(d, depth), :] = up_ref[:, :, cut(d, width)]
    for r in range(1, owners):
        wait_blocks(d, zat(r), z_s, z_r, r - 1, {"expert": zat(owners - r)})
        send_blocks(d, zat(r), x_s, x_r, r, to_x)
        send_blocks(d, zat(r), s_s, s_r, r, to_sib)

    wide = lax.broadcasted_iota(jnp.int32, (owners * block, LANES), 1)

    def inner(dd):
        gpart[dd] = jnp.zeros((owners * block, LANES), F32)

        def body(e, _):
            pre = dot(tok[dd, 0], upt[e])
            back = dot(tok[dd, 1], down_ref[cut(e, width), :], 1, 1)
            here = wide == first + e
            w = jnp.sum(jnp.where(here, tab[dd], 0.0), axis=1, keepdims=True)
            active = jnp.where(w > 0.0, jnp.maximum(pre, 0.0), 0.0)
            hidden = active * active
            gpart[dd] += jnp.where(here, jnp.sum(hidden * back, axis=1, keepdims=True), 0.0)
            gated[dd, :, cut(e, width)] = (w * hidden).astype(BF16)
            pgrad[dd, :, cut(e, width)] = (w * back * 2.0 * active).astype(BF16)
            return 0

        lax.fori_loop(0, experts, body, 0)

        def outer(n, _):
            cols = cut(n, depth)
            part[dd, 0, :, cols] = dot(gated[dd], down_ref[:, cols]).astype(BF16)
            total = jnp.zeros((owners * block, depth), F32)
            for e in range(experts):
                total += dot(pgrad[dd, :, e * width : (e + 1) * width], upt[e, cols, :], 1, 1)
            part[dd, 1, :, cols] = total.astype(BF16)
            return 0

        lax.fori_loop(0, 4, outer, 0)

    def pair_copies(i, dd):
        return (
            copy(part.at[dd], prec.at[i], p_s.at[0, i], p_r.at[0, i], to_sib),
            copy(gpart.at[dd], pgrec.at[i], p_s.at[1, i], p_r.at[1, i], to_sib),
        )

    for j in (1, 2, 3):
        m = mates[j]
        copy(up_ref.at[:, :, cut(m, width)], upt.at[:, cut(m, depth), :],
             u_s.at[j - 1], u_r.at[j - 1], {"dp": m}).wait_recv()
    for r in range(owners):
        wait_blocks(sib, zat(r), s_s, s_r, r, to_sib)
    inner(sib)
    for c in pair_copies(1, sib):
        go(c)
    for r in range(owners):
        wait_blocks(across, zat(r), x_s, x_r, r, to_x)
        send_blocks(across, zat(r), s_s, s_r, owners + r, to_sib)
    inner(d)
    for r in range(owners):
        wait_blocks(diag, zat(r), s_s, s_r, owners + r, to_sib)
    inner(diag)
    for c in pair_copies(0, diag):
        go(c)
    inner(across)
    for c in pair_copies(0, diag):
        c.wait_recv()

    order = tuple(range(1, owners)) + (0,)

    def cross_copies(r):
        rows = rows_of(zat(r))
        return (
            copy(part.at[across, :, rows, :], xrec.at[:, rows, :], y_s.at[0, r], y_r.at[0, r], to_x),
            copy(gpart.at[across, rows, :], xgrec.at[rows, :], y_s.at[1, r], y_r.at[1, r], to_x),
        )

    for r in order:
        rows = rows_of(zat(r))
        part[across, :, rows, :] = (
            part[across, :, rows, :].astype(F32) + prec[0, :, rows, :].astype(F32)
        ).astype(BF16)
        gpart[across, rows, :] += pgrec[0, rows, :]
        for c in cross_copies(r):
            go(c)

    def weight_grad(m):
        total = jnp.zeros((depth, hid), F32)
        for dd in range(4):
            total += dot(tok[dd, 0, :, cut(m, depth)], pgrad[dd], 0, 0)
        return total.astype(BF16)

    def grad_copy(j):
        return copy(gsend.at[j - 1], grec.at[j - 1], g_s.at[j - 1], g_r.at[j - 1], {"dp": mates[j]})

    def spread(m, value):
        for e in range(experts):
            gup_ref[e, :, cut(m, width)] = value[:, e * width : (e + 1) * width]

    for j in (3, 2, 1):
        gsend[j - 1] = weight_grad(mates[j])
        go(grad_copy(j))
    spread(d, weight_grad(d))
    for c in pair_copies(1, sib):
        c.wait_recv()

    def last_copies(r):
        rows = rows_of(zat(owners - r))
        where = {"expert": zat(owners - r)}
        return (
            copy(tot.at[:, rows, :], zrec.at[r - 1], w_s.at[0, r - 1], w_r.at[0, r - 1], where),
            copy(gtot.at[rows, :], zgrec.at[r - 1], w_s.at[1, r - 1], w_r.at[1, r - 1], where),
        )

    def down_grad(e):
        total = jnp.zeros((width, tok.shape[3]), F32)
        for dd in range(4):
            total += dot(gated[dd, :, e * width : (e + 1) * width], tok[dd, 1], 0, 0)
        gdown_ref[e] = total.astype(BF16)

    for i, r in enumerate(order):
        if i < experts:
            down_grad(i)
        rows = rows_of(zat(r))
        for c in cross_copies(r):
            c.wait_recv()
        tot[:, rows, :] = (
            part[d, :, rows, :].astype(F32)
            + prec[1, :, rows, :].astype(F32)
            + xrec[:, rows, :].astype(F32)
        ).astype(BF16)
        gtot[rows, :] = gpart[d, rows, :] + pgrec[1, rows, :] + xgrec[rows, :]
        if r:
            for c in last_copies(owners - r):
                go(c)
    for e in range(owners, experts):
        down_grad(e)
    for j in (1, 3, 2):
        grad_copy(j).wait_recv()
        spread(mates[j], grec[j - 1])

    both = tot[:, rows_of(z), :].astype(F32)
    gsum = gtot[rows_of(z), :]
    for r in range(1, owners):
        for c in last_copies(r):
            c.wait_recv()
        both += zrec[r - 1].astype(F32)
        gsum += zgrec[r - 1]
    out_ref[...] = both[0].astype(BF16)
    gin_ref[...] = both[1].astype(BF16)
    slots = lax.broadcasted_iota(jnp.int32, (block, tops), 1)
    found = jnp.zeros((block, tops), F32)
    for k in range(tops):
        mine = jnp.sum(jnp.where(lane == routes[:, k : k + 1], gsum, 0.0), axis=1, keepdims=True)
        found += jnp.where(slots == k, mine, 0.0)
    gate_ref[...] = found
    for c in sent:
        c.wait_send()


def by_tokens(latent_in, routes, gates, up_weight, down_weight, out_grad):
    owners = lax.axis_size("expert")
    block, latent = latent_in.shape
    experts, depth, hid = up_weight.shape
    width = hid // 4
    column = owners * block
    vmem = pltpu.VMEM
    dma = pltpu.SemaphoreType.DMA
    spec = pl.BlockSpec(memory_space=pltpu.VMEM)
    shape = jax.ShapeDtypeStruct
    out, gin, gate, gup, gdown = pl.pallas_call(
        functools.partial(kernel, owners),
        out_shape=(
            shape((block, latent), BF16),
            shape((block, latent), BF16),
            shape(gates.shape, F32),
            shape((experts, depth, hid), BF16),
            shape((experts, width, latent), BF16),
        ),
        in_specs=[spec] * 6,
        out_specs=(spec,) * 5,
        scratch_shapes=[
            vmem((4, 2, column, latent), BF16),
            vmem((4, column, LANES), F32),
            vmem((experts, latent, width), BF16),
            vmem((4, column, experts * width), BF16),
            vmem((4, column, experts * width), BF16),
            vmem((4, 2, column, latent), BF16),
            vmem((4, column, LANES), F32),
            vmem((2, 2, column, latent), BF16),
            vmem((2, column, LANES), F32),
            vmem((2, column, latent), BF16),
            vmem((column, LANES), F32),
            vmem((2, column, latent), BF16),
            vmem((column, LANES), F32),
            vmem((owners - 1, 2, block, latent), BF16),
            vmem((owners - 1, block, LANES), F32),
            vmem((3, depth, experts * width), BF16),
            vmem((3, depth, experts * width), BF16),
            dma((2, owners - 1)), dma((2, owners - 1)),
            dma((2, owners)), dma((2, owners)),
            dma((2, 2 * owners)), dma((2, 2 * owners)),
            dma((3,)), dma((3,)),
            dma((2, 2)), dma((2, 2)),
            dma((2, owners)), dma((2, owners)),
            dma((2, owners - 1)), dma((2, owners - 1)),
            dma((3,)), dma((3,)),
        ],
        compiler_params=pltpu.CompilerParams(
            collective_id=0, has_side_effects=True, vmem_limit_bytes=56 << 20
        ),
    )(latent_in, routes, gates, up_weight, down_weight.reshape(experts * width, latent), out_grad)
    return out, gin, gate, gup.astype(F32), gdown.astype(F32)


def slot_places(routes, expert_total, capacity):
    flat_ids = routes.reshape(-1)
    pair_count = flat_ids.shape[0]
    onehot = (flat_ids[:, None] == jnp.arange(expert_total, dtype=jnp.int32)[None, :]).astype(
        jnp.int32
    )
    earlier = jnp.cumsum(onehot, axis=0) - onehot
    slot_ids = jnp.sum(earlier * onehot, axis=1)
    places = flat_ids * capacity + slot_ids
    empty = jnp.full((expert_total * capacity,), pair_count, jnp.int32)
    pair_of = empty.at[places].set(jnp.arange(pair_count, dtype=jnp.int32))
    return (places, pair_of)


def by_rows(latent_in, routes, gates, up_weight, down_weight, out_grad):
    owner_count = lax.axis_size("expert")
    local_experts = up_weight.shape[0]
    expert_total = local_experts * owner_count
    token_rows, route_count = routes.shape
    latent = latent_in.shape[1]
    capacity = 9 * token_rows * route_count // (8 * expert_total)
    places, pair_of = slot_places(routes, expert_total, capacity)
    token_of = pair_of // route_count
    zero_row = jnp.zeros((1, latent), jnp.bfloat16)
    padded_in = jnp.concatenate([latent_in, zero_row], axis=0)
    padded_grad = jnp.concatenate([out_grad, zero_row], axis=0)
    padded_gates = jnp.concatenate([gates.reshape(-1), jnp.zeros((1,), jnp.float32)])
    slot_gates = padded_gates[pair_of]
    send_shape = (owner_count, local_experts * capacity, latent)
    block_shape = (owner_count, local_experts, capacity, latent)
    send_rows = padded_in[token_of].reshape(send_shape)
    send_grad = (
        (slot_gates[:, None] * padded_grad[token_of].astype(jnp.float32))
        .astype(jnp.bfloat16)
        .reshape(send_shape)
    )
    up_full, down_full = (
        lax.all_gather(up_weight, "dp", axis=1, tiled=True),
        lax.all_gather(down_weight, "dp", axis=1, tiled=True),
    )
    arrived = lax.all_to_all(send_rows, "expert", split_axis=0, concat_axis=0, tiled=True)
    forward_rows_four = arrived.reshape(block_shape)
    pre_act = jnp.einsum(
        "secl,elh->sech", forward_rows_four, up_full, preferred_element_type=jnp.float32
    )
    active = jnp.maximum(pre_act, 0.0)
    forward_hidden = (active * active).astype(jnp.bfloat16)
    result = jnp.einsum(
        "sech,ehl->secl", forward_hidden, down_full, preferred_element_type=jnp.float32
    ).astype(jnp.bfloat16)
    rows_four, active, hidden, result = (
        forward_rows_four,
        active,
        forward_hidden,
        result.reshape(send_shape),
    )
    returned = lax.all_to_all(result, "expert", split_axis=0, concat_axis=0, tiled=True)
    arrived_grad = lax.all_to_all(send_grad, "expert", split_axis=0, concat_axis=0, tiled=True)
    backward_grad_four = arrived_grad.reshape(block_shape)
    hidden_grad = jnp.einsum(
        "secl,ehl->sech", backward_grad_four, down_full, preferred_element_type=jnp.float32
    )
    backward_pre_grad = (hidden_grad * 2.0 * active).astype(jnp.bfloat16)
    row_grad = jnp.einsum(
        "sech,elh->secl", backward_pre_grad, up_full, preferred_element_type=jnp.float32
    ).astype(jnp.bfloat16)
    grad_four, pre_grad, row_grad = (
        backward_grad_four,
        backward_pre_grad,
        row_grad.reshape(send_shape),
    )
    returned_grad = lax.all_to_all(row_grad, "expert", split_axis=0, concat_axis=0, tiled=True)
    picked = (
        returned.reshape(expert_total * capacity, latent)[places]
        .reshape(token_rows, route_count, latent)
        .astype(jnp.float32)
    )
    latent_out = jnp.sum(gates[:, :, None] * picked, axis=1).astype(jnp.bfloat16)
    gate_grad = jnp.sum(out_grad.astype(jnp.float32)[:, None, :] * picked, axis=2)
    picked_grad = (
        returned_grad.reshape(expert_total * capacity, latent)[places]
        .reshape(token_rows, route_count, latent)
        .astype(jnp.float32)
    )
    grad_in = jnp.sum(picked_grad, axis=1).astype(jnp.bfloat16)
    up_sum = lax.psum_scatter(
        jnp.einsum(
            "secl,sech->leh", rows_four, pre_grad, preferred_element_type=jnp.float32
        ).astype(jnp.bfloat16),
        "dp",
        scatter_dimension=0,
        tiled=True,
    ).astype(jnp.float32)
    down_sum = lax.psum_scatter(
        jnp.einsum("sech,secl->hel", hidden, grad_four, preferred_element_type=jnp.float32).astype(
            jnp.bfloat16
        ),
        "dp",
        scatter_dimension=0,
        tiled=True,
    ).astype(jnp.float32)
    grad_up = jnp.transpose(up_sum, (1, 0, 2))
    grad_down = jnp.transpose(down_sum, (1, 0, 2))
    return (latent_out, grad_in, gate_grad, grad_up, grad_down)


def local(*args):
    owners, parts = lax.axis_size("expert"), lax.axis_size("dp")
    block, latent = args[0].shape
    experts, depth, hid = args[3].shape
    square = parts == 4 and hid == latent and depth * 4 == hid and hid % 512 == 0
    small = block * owners * parts <= 1024 and latent <= 1024 and experts * owners <= LANES
    if square and small and experts == 4 and owners > 1 and block % 16 == 0:
        return by_tokens(*args)
    return by_rows(*args)


def solution(mesh):
    tokens = P(("group", "expert", "dp"), None)
    weights = P("expert", "dp", None)
    grads = P(("group", "expert"), "dp", None)
    return jax.shard_map(
        local,
        mesh=mesh,
        in_specs=(tokens, tokens, tokens, weights, weights, tokens),
        out_specs=(tokens, tokens, tokens, grads, grads),
        check_vma=False,
    )
```

```python
import functools

import jax
import jax.numpy as jnp
from jax import lax
from jax.experimental import pallas as pl
from jax.experimental.pallas import tpu as pltpu
from jax.sharding import PartitionSpec as P

BF16, F32 = jnp.bfloat16, jnp.float32
LANES = 128


def dot(a, b, left=1, right=0):
    return lax.dot_general(a, b, (((left,), (right,)), ((), ())), preferred_element_type=F32)


def kernel(
    owners, lat_ref, routes_ref, gates_ref, up_ref, down_ref, dy_ref,
    out_ref, gin_ref, gate_ref, gup_ref, gdown_ref,
    tok, tab, upt, gated, pgrad, part, gpart, prec, pgrec, xrec, xgrec, tot, gtot, zrec, zgrec,
    gsend, grec,
    z_s, z_r, x_s, x_r, s_s, s_r, u_s, u_r, v_s, v_r, p_s, p_r, y_s, y_r, w_s, w_r, g_s, g_r,
):
    block = lat_ref.shape[0]
    experts, depth, hid = up_ref.shape
    width = hid // 4
    z, d = lax.axis_index("expert"), lax.axis_index("dp")
    group = lax.axis_index("group")
    half = experts // 2
    my_half, other_half = pl.ds(group * half, half), pl.ds((1 - group) * half, half)
    to_twin = {"group": 1 - group}
    sib, across, diag = d + 1 - 2 * (d % 2), (d + 2) % 4, 3 - d
    mates = (d, sib, across, diag)
    first = z * experts

    def zat(r):
        return (z + r) % owners

    def rows_of(zs):
        return pl.ds(pl.multiple_of(zs * block, block), block)

    def cut(i, size):
        return pl.ds(pl.multiple_of(i * size, size), size)

    def copy(src, dst, send, recv, where):
        return pltpu.make_async_remote_copy(
            src_ref=src, dst_ref=dst, send_sem=send, recv_sem=recv,
            device_id=where, device_id_type=pl.DeviceIdType.MESH,
        )

    sent = []

    def go(c):
        c.start()
        sent.append(c)

    barrier = pltpu.get_barrier_semaphore()
    for m in mates[1:]:
        pl.semaphore_signal(barrier, inc=1, device_id={"dp": m}, device_id_type=pl.DeviceIdType.MESH)
    for r in range(1, owners):
        pl.semaphore_signal(
            barrier, inc=1, device_id={"expert": zat(r)}, device_id_type=pl.DeviceIdType.MESH
        )

    pl.semaphore_signal(barrier, inc=1, device_id=to_twin, device_id_type=pl.DeviceIdType.MESH)

    lane = lax.broadcasted_iota(jnp.int32, (block, LANES), 1)
    routes, gates = jnp.transpose(routes_ref[...]), jnp.transpose(gates_ref[...])
    tops = routes.shape[1]
    table = jnp.zeros((block, LANES), F32)
    for k in range(tops):
        table += jnp.where(lane == routes[:, k : k + 1], gates[:, k : k + 1], 0.0)
    tok[d, 0, rows_of(z), :] = lat_ref[...]
    tok[d, 1, rows_of(z), :] = dy_ref[...]
    tab[d, rows_of(z), :] = table
    pl.semaphore_wait(barrier, 3 + owners - 1 + 1)

    def blocks(dd, zs, send, recv, i, where):
        a, b = tok.at[dd, :, rows_of(zs), :], tab.at[dd, rows_of(zs), :]
        return (
            copy(a, a, send.at[0, i], recv.at[0, i], where),
            copy(b, b, send.at[1, i], recv.at[1, i], where),
        )

    def send_blocks(*args):
        for c in blocks(*args):
            go(c)

    def wait_blocks(*args):
        for c in blocks(*args):
            c.wait_recv()

    to_sib, to_x = {"dp": sib}, {"dp": across}
    for r in range(1, owners):
        send_blocks(d, z, z_s, z_r, r - 1, {"expert": zat(owners - r)})
    send_blocks(d, z, x_s, x_r, 0, to_x)
    send_blocks(d, z, s_s, s_r, 0, to_sib)

    def up_copy(j, source, target):
        m = mates[j]
        es = slice(None) if j == 1 else my_half
        return copy(up_ref.at[es, :, cut(target, width)], upt.at[es, cut(source, depth), :],
                    u_s.at[j - 1], u_r.at[j - 1], {"dp": m})

    def twin_copy(j, es):
        part_of = upt.at[es, cut(mates[j], depth), :]
        return copy(part_of, part_of, v_s.at[j - 2], v_r.at[j - 2], to_twin)

    for j in (2, 3, 1):
        go(up_copy(j, d, mates[j]))
    upt[:, cut(d, depth), :] = up_ref[:, :, cut(d, width)]
    for r in range(1, owners):
        wait_blocks(d, zat(r), z_s, z_r, r - 1, {"expert": zat(owners - r)})
        send_blocks(d, zat(r), x_s, x_r, r, to_x)
        send_blocks(d, zat(r), s_s, s_r, r, to_sib)
        if r == min(2, owners - 1):
            for j in (2, 3):
                up_copy(j, mates[j], d).wait_recv()
                go(twin_copy(j, my_half))

    wide = lax.broadcasted_iota(jnp.int32, (owners * block, LANES), 1)

    def activate(dd):
        gpart[dd] = jnp.zeros((owners * block, LANES), F32)

        def body(e, _):
            pre = dot(tok[dd, 0], upt[e])
            back = dot(tok[dd, 1], down_ref[cut(e, width), :], 1, 1)
            here = wide == first + e
            w = jnp.sum(jnp.where(here, tab[dd], 0.0), axis=1, keepdims=True)
            active = jnp.where(w > 0.0, jnp.maximum(pre, 0.0), 0.0)
            hidden = active * active
            gpart[dd] += jnp.where(here, jnp.sum(hidden * back, axis=1, keepdims=True), 0.0)
            gated[dd, :, cut(e, width)] = (w * hidden).astype(BF16)
            pgrad[dd, :, cut(e, width)] = (w * back * 2.0 * active).astype(BF16)
            return 0

        lax.fori_loop(0, experts, body, 0)

    def project(dd):
        def outer(n, _):
            cols = cut(n, depth)
            part[dd, 0, :, cols] = dot(gated[dd], down_ref[:, cols]).astype(BF16)
            total = jnp.zeros((owners * block, depth), F32)
            for e in range(experts):
                total += dot(pgrad[dd, :, e * width : (e + 1) * width], upt[e, cols, :], 1, 1)
            part[dd, 1, :, cols] = total.astype(BF16)
            return 0

        lax.fori_loop(0, 4, outer, 0)

    def pair_copies(i, dd):
        return (
            copy(part.at[dd], prec.at[i], p_s.at[0, i], p_r.at[0, i], to_sib),
            copy(gpart.at[dd], pgrec.at[i], p_s.at[1, i], p_r.at[1, i], to_sib),
        )

    up_copy(1, sib, d).wait_recv()
    for j in (2, 3):
        twin_copy(j, other_half).wait_recv()
    activate(d)
    project(d)
    for r in range(owners):
        wait_blocks(across, zat(r), x_s, x_r, r, to_x)
        send_blocks(across, zat(r), s_s, s_r, owners + r, to_sib)
    activate(across)
    for r in range(owners):
        wait_blocks(diag, zat(r), s_s, s_r, owners + r, to_sib)
    activate(diag)
    project(diag)
    for c in pair_copies(0, diag):
        go(c)
    project(across)
    for r in range(owners):
        wait_blocks(sib, zat(r), s_s, s_r, r, to_sib)
    activate(sib)
    for c in pair_copies(0, diag):
        c.wait_recv()

    order = tuple(range(1, owners)) + (0,)

    def cross_copies(r):
        rows = rows_of(zat(r))
        return (
            copy(part.at[across, :, rows, :], xrec.at[:, rows, :], y_s.at[0, r], y_r.at[0, r], to_x),
            copy(gpart.at[across, rows, :], xgrec.at[rows, :], y_s.at[1, r], y_r.at[1, r], to_x),
        )

    for r in order:
        rows = rows_of(zat(r))
        part[across, :, rows, :] = (
            part[across, :, rows, :].astype(F32) + prec[0, :, rows, :].astype(F32)
        ).astype(BF16)
        gpart[across, rows, :] += pgrec[0, rows, :]
        for c in cross_copies(r):
            go(c)

    def weight_grad(m):
        total = jnp.zeros((depth, hid), F32)
        for dd in range(4):
            total += dot(tok[dd, 0, :, cut(m, depth)], pgrad[dd], 0, 0)
        return total.astype(BF16)

    def grad_copy(j):
        return copy(gsend.at[j - 1], grec.at[j - 1], g_s.at[j - 1], g_r.at[j - 1], {"dp": mates[j]})

    def spread(m, value):
        for e in range(experts):
            gup_ref[e, :, cut(m, width)] = value[:, e * width : (e + 1) * width]

    project(sib)
    for c in pair_copies(1, sib):
        go(c)
    for j in (3, 2, 1):
        gsend[j - 1] = weight_grad(mates[j])
    go(grad_copy(1))
    spread(d, weight_grad(d))
    for c in pair_copies(1, sib):
        c.wait_recv()

    def last_copies(r):
        rows = rows_of(zat(owners - r))
        where = {"expert": zat(owners - r)}
        return (
            copy(tot.at[:, rows, :], zrec.at[r - 1], w_s.at[0, r - 1], w_r.at[0, r - 1], where),
            copy(gtot.at[rows, :], zgrec.at[r - 1], w_s.at[1, r - 1], w_r.at[1, r - 1], where),
        )

    def down_grad(e):
        total = jnp.zeros((width, tok.shape[3]), F32)
        for dd in range(4):
            total += dot(gated[dd, :, e * width : (e + 1) * width], tok[dd, 1], 0, 0)
        gdown_ref[e] = total.astype(BF16)

    for i, r in enumerate(order):
        if i < experts:
            down_grad(i)
        rows = rows_of(zat(r))
        for c in cross_copies(r):
            c.wait_recv()
        if i == min(1, owners - 1):
            go(grad_copy(3))
        if i == min(2, owners - 1):
            go(grad_copy(2))
        tot[:, rows, :] = (
            part[d, :, rows, :].astype(F32)
            + prec[1, :, rows, :].astype(F32)
            + xrec[:, rows, :].astype(F32)
        ).astype(BF16)
        gtot[rows, :] = gpart[d, rows, :] + pgrec[1, rows, :] + xgrec[rows, :]
        if r:
            for c in last_copies(owners - r):
                go(c)
    for e in range(owners, experts):
        down_grad(e)
    grad_copy(1).wait_recv()
    spread(sib, grec[0])

    both = tot[:, rows_of(z), :].astype(F32)
    gsum = gtot[rows_of(z), :]
    for r in range(1, owners):
        for c in last_copies(r):
            c.wait_recv()
        both += zrec[r - 1].astype(F32)
        gsum += zgrec[r - 1]
    out_ref[...] = both[0].astype(BF16)
    gin_ref[...] = both[1].astype(BF16)
    slots = lax.broadcasted_iota(jnp.int32, (block, tops), 1)
    found = jnp.zeros((block, tops), F32)
    for k in range(tops):
        mine = jnp.sum(jnp.where(lane == routes[:, k : k + 1], gsum, 0.0), axis=1, keepdims=True)
        found += jnp.where(slots == k, mine, 0.0)
    gate_ref[...] = jnp.transpose(found)
    for j in (3, 2):
        grad_copy(j).wait_recv()
        spread(mates[j], grec[j - 1])
    for c in sent:
        c.wait_send()


def by_tokens(latent_in, routes, gates, up_weight, down_weight, out_grad):
    owners = lax.axis_size("expert")
    block, latent = latent_in.shape
    experts, depth, hid = up_weight.shape
    width = hid // 4
    column = owners * block
    vmem = pltpu.VMEM
    dma = pltpu.SemaphoreType.DMA
    spec = pl.BlockSpec(memory_space=pltpu.VMEM)
    shape = jax.ShapeDtypeStruct
    out, gin, gate, gup, gdown = pl.pallas_call(
        functools.partial(kernel, owners),
        out_shape=(
            shape((block, latent), BF16),
            shape((block, latent), BF16),
            shape(gates.shape[::-1], F32),
            shape((experts, depth, hid), BF16),
            shape((experts, width, latent), BF16),
        ),
        in_specs=[spec] * 6,
        out_specs=(spec,) * 5,
        scratch_shapes=[
            vmem((4, 2, column, latent), BF16),
            vmem((4, column, LANES), F32),
            vmem((experts, latent, width), BF16),
            vmem((4, column, experts * width), BF16),
            vmem((4, column, experts * width), BF16),
            vmem((4, 2, column, latent), BF16),
            vmem((4, column, LANES), F32),
            vmem((2, 2, column, latent), BF16),
            vmem((2, column, LANES), F32),
            vmem((2, column, latent), BF16),
            vmem((column, LANES), F32),
            vmem((2, column, latent), BF16),
            vmem((column, LANES), F32),
            vmem((owners - 1, 2, block, latent), BF16),
            vmem((owners - 1, block, LANES), F32),
            vmem((3, depth, experts * width), BF16),
            vmem((3, depth, experts * width), BF16),
            dma((2, owners - 1)), dma((2, owners - 1)),
            dma((2, owners)), dma((2, owners)),
            dma((2, 2 * owners)), dma((2, 2 * owners)),
            dma((3,)), dma((3,)),
            dma((2,)), dma((2,)),
            dma((2, 2)), dma((2, 2)),
            dma((2, owners)), dma((2, owners)),
            dma((2, owners - 1)), dma((2, owners - 1)),
            dma((3,)), dma((3,)),
        ],
        compiler_params=pltpu.CompilerParams(
            collective_id=0, has_side_effects=True, vmem_limit_bytes=56 << 20
        ),
    )(
        latent_in, routes.T, gates.T, up_weight,
        down_weight.reshape(experts * width, latent), out_grad,
    )
    return out, gin, gate.T, gup.astype(F32), gdown.astype(F32)


def slot_places(routes, expert_total, capacity):
    flat_ids = routes.reshape(-1)
    pair_count = flat_ids.shape[0]
    onehot = (flat_ids[:, None] == jnp.arange(expert_total, dtype=jnp.int32)[None, :]).astype(
        jnp.int32
    )
    earlier = jnp.cumsum(onehot, axis=0) - onehot
    slot_ids = jnp.sum(earlier * onehot, axis=1)
    places = flat_ids * capacity + slot_ids
    empty = jnp.full((expert_total * capacity,), pair_count, jnp.int32)
    pair_of = empty.at[places].set(jnp.arange(pair_count, dtype=jnp.int32))
    return (places, pair_of)


def by_rows(latent_in, routes, gates, up_weight, down_weight, out_grad):
    owner_count = lax.axis_size("expert")
    local_experts = up_weight.shape[0]
    expert_total = local_experts * owner_count
    token_rows, route_count = routes.shape
    latent = latent_in.shape[1]
    capacity = 9 * token_rows * route_count // (8 * expert_total)
    places, pair_of = slot_places(routes, expert_total, capacity)
    token_of = pair_of // route_count
    zero_row = jnp.zeros((1, latent), jnp.bfloat16)
    padded_in = jnp.concatenate([latent_in, zero_row], axis=0)
    padded_grad = jnp.concatenate([out_grad, zero_row], axis=0)
    padded_gates = jnp.concatenate([gates.reshape(-1), jnp.zeros((1,), jnp.float32)])
    slot_gates = padded_gates[pair_of]
    send_shape = (owner_count, local_experts * capacity, latent)
    block_shape = (owner_count, local_experts, capacity, latent)
    send_rows = padded_in[token_of].reshape(send_shape)
    send_grad = (
        (slot_gates[:, None] * padded_grad[token_of].astype(jnp.float32))
        .astype(jnp.bfloat16)
        .reshape(send_shape)
    )
    up_full, down_full = (
        lax.all_gather(up_weight, "dp", axis=1, tiled=True),
        lax.all_gather(down_weight, "dp", axis=1, tiled=True),
    )
    arrived = lax.all_to_all(send_rows, "expert", split_axis=0, concat_axis=0, tiled=True)
    forward_rows_four = arrived.reshape(block_shape)
    pre_act = jnp.einsum(
        "secl,elh->sech", forward_rows_four, up_full, preferred_element_type=jnp.float32
    )
    active = jnp.maximum(pre_act, 0.0)
    forward_hidden = (active * active).astype(jnp.bfloat16)
    result = jnp.einsum(
        "sech,ehl->secl", forward_hidden, down_full, preferred_element_type=jnp.float32
    ).astype(jnp.bfloat16)
    rows_four, active, hidden, result = (
        forward_rows_four,
        active,
        forward_hidden,
        result.reshape(send_shape),
    )
    returned = lax.all_to_all(result, "expert", split_axis=0, concat_axis=0, tiled=True)
    arrived_grad = lax.all_to_all(send_grad, "expert", split_axis=0, concat_axis=0, tiled=True)
    backward_grad_four = arrived_grad.reshape(block_shape)
    hidden_grad = jnp.einsum(
        "secl,ehl->sech", backward_grad_four, down_full, preferred_element_type=jnp.float32
    )
    backward_pre_grad = (hidden_grad * 2.0 * active).astype(jnp.bfloat16)
    row_grad = jnp.einsum(
        "sech,elh->secl", backward_pre_grad, up_full, preferred_element_type=jnp.float32
    ).astype(jnp.bfloat16)
    grad_four, pre_grad, row_grad = (
        backward_grad_four,
        backward_pre_grad,
        row_grad.reshape(send_shape),
    )
    returned_grad = lax.all_to_all(row_grad, "expert", split_axis=0, concat_axis=0, tiled=True)
    picked = (
        returned.reshape(expert_total * capacity, latent)[places]
        .reshape(token_rows, route_count, latent)
        .astype(jnp.float32)
    )
    latent_out = jnp.sum(gates[:, :, None] * picked, axis=1).astype(jnp.bfloat16)
    gate_grad = jnp.sum(out_grad.astype(jnp.float32)[:, None, :] * picked, axis=2)
    picked_grad = (
        returned_grad.reshape(expert_total * capacity, latent)[places]
        .reshape(token_rows, route_count, latent)
        .astype(jnp.float32)
    )
    grad_in = jnp.sum(picked_grad, axis=1).astype(jnp.bfloat16)
    up_sum = lax.psum_scatter(
        jnp.einsum(
            "secl,sech->leh", rows_four, pre_grad, preferred_element_type=jnp.float32
        ).astype(jnp.bfloat16),
        "dp",
        scatter_dimension=0,
        tiled=True,
    ).astype(jnp.float32)
    down_sum = lax.psum_scatter(
        jnp.einsum("sech,secl->hel", hidden, grad_four, preferred_element_type=jnp.float32).astype(
            jnp.bfloat16
        ),
        "dp",
        scatter_dimension=0,
        tiled=True,
    ).astype(jnp.float32)
    grad_up = jnp.transpose(up_sum, (1, 0, 2))
    grad_down = jnp.transpose(down_sum, (1, 0, 2))
    return (latent_out, grad_in, gate_grad, grad_up, grad_down)


def local(*args):
    owners, parts = lax.axis_size("expert"), lax.axis_size("dp")
    block, latent = args[0].shape
    experts, depth, hid = args[3].shape
    square = parts == 4 and lax.axis_size("group") == 2 and hid == latent and depth * 4 == hid and hid % 512 == 0
    small = block * owners * parts <= 1024 and latent <= 1024 and experts * owners <= LANES
    if square and small and experts == 4 and owners > 1 and block % 16 == 0:
        return by_tokens(*args)
    return by_rows(*args)


def solution(mesh):
    tokens = P(("group", "expert", "dp"), None)
    weights = P("expert", "dp", None)
    grads = P(("group", "expert"), "dp", None)
    return jax.shard_map(
        local,
        mesh=mesh,
        in_specs=(tokens, tokens, tokens, weights, weights, tokens),
        out_specs=(tokens, tokens, tokens, grads, grads),
        check_vma=False,
    )
```

```python
import functools

import jax
import jax.numpy as jnp
from jax import lax
from jax.experimental import pallas as pl
from jax.experimental.pallas import tpu as pltpu
from jax.sharding import PartitionSpec as P

BF16, F32 = jnp.bfloat16, jnp.float32
LANES = 128


def dot(a, b, left=1, right=0):
    return lax.dot_general(a, b, (((left,), (right,)), ((), ())), preferred_element_type=F32)


def kernel(
    owners, lat_ref, routes_ref, gates_ref, up_ref, down_ref, dy_ref,
    out_ref, gin_ref, gate_ref, gup_ref, gdown_ref,
    tok, tab, upt, gated, pgrad, part, gpart, prec, pgrec, xrec, xgrec, tot, gtot, zrec, zgrec,
    gsend, grec,
    z_s, z_r, x_s, x_r, s_s, s_r, u_s, u_r, v_s, v_r, p_s, p_r, y_s, y_r, w_s, w_r, g_s, g_r,
):
    block = lat_ref.shape[0]
    experts, depth, hid = up_ref.shape
    width = hid // 4
    z, d = lax.axis_index("expert"), lax.axis_index("dp")
    group = lax.axis_index("group")
    half = experts // 2
    my_half, other_half = pl.ds(group * half, half), pl.ds((1 - group) * half, half)
    to_twin = {"group": 1 - group}
    sib, across, diag = d + 1 - 2 * (d % 2), (d + 2) % 4, 3 - d
    mates = (d, sib, across, diag)
    first = z * experts

    def zat(r):
        return (z + r) % owners

    def rows_of(zs):
        return pl.ds(pl.multiple_of(zs * block, block), block)

    def cut(i, size):
        return pl.ds(pl.multiple_of(i * size, size), size)

    def copy(src, dst, send, recv, where):
        return pltpu.make_async_remote_copy(
            src_ref=src, dst_ref=dst, send_sem=send, recv_sem=recv,
            device_id=where, device_id_type=pl.DeviceIdType.MESH,
        )

    sent = []

    def go(c):
        c.start()
        sent.append(c)

    barrier = pltpu.get_barrier_semaphore()
    for m in mates[1:]:
        pl.semaphore_signal(barrier, inc=1, device_id={"dp": m}, device_id_type=pl.DeviceIdType.MESH)
    for r in range(1, owners):
        pl.semaphore_signal(
            barrier, inc=1, device_id={"expert": zat(r)}, device_id_type=pl.DeviceIdType.MESH
        )

    pl.semaphore_signal(barrier, inc=1, device_id=to_twin, device_id_type=pl.DeviceIdType.MESH)

    lane = lax.broadcasted_iota(jnp.int32, (block, LANES), 1)
    routes, gates = jnp.transpose(routes_ref[...]), jnp.transpose(gates_ref[...])
    tops = routes.shape[1]
    table = jnp.zeros((block, LANES), F32)
    for k in range(tops):
        table += jnp.where(lane == routes[:, k : k + 1], gates[:, k : k + 1], 0.0)
    tok[d, 0, rows_of(z), :] = lat_ref[...]
    tok[d, 1, rows_of(z), :] = dy_ref[...]
    tab[d, rows_of(z), :] = table
    pl.semaphore_wait(barrier, 3 + owners - 1 + 1)

    def blocks(dd, zs, send, recv, i, where):
        a, b = tok.at[dd, :, rows_of(zs), :], tab.at[dd, rows_of(zs), :]
        return (
            copy(a, a, send.at[0, i], recv.at[0, i], where),
            copy(b, b, send.at[1, i], recv.at[1, i], where),
        )

    def send_blocks(*args):
        for c in blocks(*args):
            go(c)

    def wait_blocks(*args):
        for c in blocks(*args):
            c.wait_recv()

    to_sib, to_x = {"dp": sib}, {"dp": across}
    for r in range(1, owners):
        send_blocks(d, z, z_s, z_r, r - 1, {"expert": zat(owners - r)})
    send_blocks(d, z, x_s, x_r, 0, to_x)
    send_blocks(d, z, s_s, s_r, 0, to_sib)

    def up_copy(j, source, target):
        m = mates[j]
        es = slice(None) if j == 1 else my_half
        return copy(up_ref.at[es, :, cut(target, width)], upt.at[es, cut(source, depth), :],
                    u_s.at[j - 1], u_r.at[j - 1], {"dp": m})

    def twin_copy(j, es):
        part_of = upt.at[es, cut(mates[j], depth), :]
        return copy(part_of, part_of, v_s.at[j - 2], v_r.at[j - 2], to_twin)

    for j in (2, 3, 1):
        go(up_copy(j, d, mates[j]))
    upt[:, cut(d, depth), :] = up_ref[:, :, cut(d, width)]
    for r in range(1, owners):
        wait_blocks(d, zat(r), z_s, z_r, r - 1, {"expert": zat(owners - r)})
        send_blocks(d, zat(r), x_s, x_r, r, to_x)
        send_blocks(d, zat(r), s_s, s_r, r, to_sib)
        if r == min(2, owners - 1):
            for j in (2, 3):
                up_copy(j, mates[j], d).wait_recv()
                go(twin_copy(j, my_half))

    wide = lax.broadcasted_iota(jnp.int32, (owners * block, LANES), 1)

    def activate(dd):
        gpart[dd] = jnp.zeros((owners * block, LANES), F32)

        def body(e, _):
            pre = dot(tok[dd, 0], upt[e])
            back = dot(tok[dd, 1], down_ref[cut(e, width), :], 1, 1)
            here = wide == first + e
            w = jnp.sum(jnp.where(here, tab[dd], 0.0), axis=1, keepdims=True)
            active = jnp.where(w > 0.0, jnp.maximum(pre, 0.0), 0.0)
            hidden = active * active
            gpart[dd] += jnp.where(here, jnp.sum(hidden * back, axis=1, keepdims=True), 0.0)
            gated[dd, :, cut(e, width)] = (w * hidden).astype(BF16)
            pgrad[dd, :, cut(e, width)] = (w * back * 2.0 * active).astype(BF16)
            return 0

        lax.fori_loop(0, experts, body, 0)

    def project(dd):
        def outer(n, _):
            cols = cut(n, depth)
            part[dd, 0, :, cols] = dot(gated[dd], down_ref[:, cols]).astype(BF16)
            total = jnp.zeros((owners * block, depth), F32)
            for e in range(experts):
                total += dot(pgrad[dd, :, e * width : (e + 1) * width], upt[e, cols, :], 1, 1)
            part[dd, 1, :, cols] = total.astype(BF16)
            return 0

        lax.fori_loop(0, 4, outer, 0)

    def pair_copies(i, dd):
        return (
            copy(part.at[dd], prec.at[i], p_s.at[0, i], p_r.at[0, i], to_sib),
            copy(gpart.at[dd], pgrec.at[i], p_s.at[1, i], p_r.at[1, i], to_sib),
        )

    up_copy(1, sib, d).wait_recv()
    for j in (2, 3):
        twin_copy(j, other_half).wait_recv()
    activate(d)
    project(d)
    for r in range(owners):
        wait_blocks(across, zat(r), x_s, x_r, r, to_x)
        send_blocks(across, zat(r), s_s, s_r, owners + r, to_sib)
    activate(across)
    for r in range(owners):
        wait_blocks(diag, zat(r), s_s, s_r, owners + r, to_sib)
    activate(diag)
    project(diag)
    for c in pair_copies(0, diag):
        go(c)
    project(across)
    for c in pair_copies(0, diag):
        c.wait_recv()

    order = tuple(range(1, owners)) + (0,)

    def cross_copies(r):
        rows = rows_of(zat(r))
        return (
            copy(part.at[across, :, rows, :], xrec.at[:, rows, :], y_s.at[0, r], y_r.at[0, r], to_x),
            copy(gpart.at[across, rows, :], xgrec.at[rows, :], y_s.at[1, r], y_r.at[1, r], to_x),
        )

    for r in order:
        rows = rows_of(zat(r))
        part[across, :, rows, :] = (
            part[across, :, rows, :].astype(F32) + prec[0, :, rows, :].astype(F32)
        ).astype(BF16)
        gpart[across, rows, :] += pgrec[0, rows, :]
        for c in cross_copies(r):
            go(c)

    def weight_grad(m):
        total = jnp.zeros((depth, hid), F32)
        for dd in range(4):
            total += dot(tok[dd, 0, :, cut(m, depth)], pgrad[dd], 0, 0)
        return total.astype(BF16)

    def grad_copy(j):
        return copy(gsend.at[j - 1], grec.at[j - 1], g_s.at[j - 1], g_r.at[j - 1], {"dp": mates[j]})

    def spread(m, value):
        for e in range(experts):
            gup_ref[e, :, cut(m, width)] = value[:, e * width : (e + 1) * width]

    for r in range(owners):
        wait_blocks(sib, zat(r), s_s, s_r, r, to_sib)
    activate(sib)
    project(sib)
    for c in pair_copies(1, sib):
        go(c)
    for j in (3, 2, 1):
        gsend[j - 1] = weight_grad(mates[j])
    go(grad_copy(1))
    spread(d, weight_grad(d))
    for c in pair_copies(1, sib):
        c.wait_recv()

    def last_copies(r):
        rows = rows_of(zat(owners - r))
        where = {"expert": zat(owners - r)}
        return (
            copy(tot.at[:, rows, :], zrec.at[r - 1], w_s.at[0, r - 1], w_r.at[0, r - 1], where),
            copy(gtot.at[rows, :], zgrec.at[r - 1], w_s.at[1, r - 1], w_r.at[1, r - 1], where),
        )

    def down_grad(e):
        total = jnp.zeros((width, tok.shape[3]), F32)
        for dd in range(4):
            total += dot(gated[dd, :, e * width : (e + 1) * width], tok[dd, 1], 0, 0)
        gdown_ref[e] = total.astype(BF16)

    for i, r in enumerate(order):
        if i < experts:
            down_grad(i)
        rows = rows_of(zat(r))
        for c in cross_copies(r):
            c.wait_recv()
        if i == min(1, owners - 1):
            go(grad_copy(3))
        if i == min(2, owners - 1):
            go(grad_copy(2))
        tot[:, rows, :] = (
            part[d, :, rows, :].astype(F32)
            + prec[1, :, rows, :].astype(F32)
            + xrec[:, rows, :].astype(F32)
        ).astype(BF16)
        gtot[rows, :] = gpart[d, rows, :] + pgrec[1, rows, :] + xgrec[rows, :]
        if r:
            for c in last_copies(owners - r):
                go(c)
    for e in range(owners, experts):
        down_grad(e)
    grad_copy(1).wait_recv()
    spread(sib, grec[0])

    both = tot[:, rows_of(z), :].astype(F32)
    gsum = gtot[rows_of(z), :]
    for r in range(1, owners):
        for c in last_copies(r):
            c.wait_recv()
        both += zrec[r - 1].astype(F32)
        gsum += zgrec[r - 1]
    out_ref[...] = both[0].astype(BF16)
    gin_ref[...] = both[1].astype(BF16)
    slots = lax.broadcasted_iota(jnp.int32, (block, tops), 1)
    found = jnp.zeros((block, tops), F32)
    for k in range(tops):
        mine = jnp.sum(jnp.where(lane == routes[:, k : k + 1], gsum, 0.0), axis=1, keepdims=True)
        found += jnp.where(slots == k, mine, 0.0)
    gate_ref[...] = jnp.transpose(found)
    for j in (3, 2):
        grad_copy(j).wait_recv()
        spread(mates[j], grec[j - 1])
    for c in sent:
        c.wait_send()


def by_tokens(latent_in, routes, gates, up_weight, down_weight, out_grad):
    owners = lax.axis_size("expert")
    block, latent = latent_in.shape
    experts, depth, hid = up_weight.shape
    width = hid // 4
    column = owners * block
    vmem = pltpu.VMEM
    dma = pltpu.SemaphoreType.DMA
    spec = pl.BlockSpec(memory_space=pltpu.VMEM)
    shape = jax.ShapeDtypeStruct
    out, gin, gate, gup, gdown = pl.pallas_call(
        functools.partial(kernel, owners),
        out_shape=(
            shape((block, latent), BF16),
            shape((block, latent), BF16),
            shape(gates.shape[::-1], F32),
            shape((experts, depth, hid), BF16),
            shape((experts, width, latent), BF16),
        ),
        in_specs=[spec] * 6,
        out_specs=(spec,) * 5,
        scratch_shapes=[
            vmem((4, 2, column, latent), BF16),
            vmem((4, column, LANES), F32),
            vmem((experts, latent, width), BF16),
            vmem((4, column, experts * width), BF16),
            vmem((4, column, experts * width), BF16),
            vmem((4, 2, column, latent), BF16),
            vmem((4, column, LANES), F32),
            vmem((2, 2, column, latent), BF16),
            vmem((2, column, LANES), F32),
            vmem((2, column, latent), BF16),
            vmem((column, LANES), F32),
            vmem((2, column, latent), BF16),
            vmem((column, LANES), F32),
            vmem((owners - 1, 2, block, latent), BF16),
            vmem((owners - 1, block, LANES), F32),
            vmem((3, depth, experts * width), BF16),
            vmem((3, depth, experts * width), BF16),
            dma((2, owners - 1)), dma((2, owners - 1)),
            dma((2, owners)), dma((2, owners)),
            dma((2, 2 * owners)), dma((2, 2 * owners)),
            dma((3,)), dma((3,)),
            dma((2,)), dma((2,)),
            dma((2, 2)), dma((2, 2)),
            dma((2, owners)), dma((2, owners)),
            dma((2, owners - 1)), dma((2, owners - 1)),
            dma((3,)), dma((3,)),
        ],
        compiler_params=pltpu.CompilerParams(
            collective_id=0, has_side_effects=True, vmem_limit_bytes=56 << 20
        ),
    )(
        latent_in, routes.T, gates.T, up_weight,
        down_weight.reshape(experts * width, latent), out_grad,
    )
    return out, gin, gate.T, gup.astype(F32), gdown.astype(F32)


def slot_places(routes, expert_total, capacity):
    flat_ids = routes.reshape(-1)
    pair_count = flat_ids.shape[0]
    onehot = (flat_ids[:, None] == jnp.arange(expert_total, dtype=jnp.int32)[None, :]).astype(
        jnp.int32
    )
    earlier = jnp.cumsum(onehot, axis=0) - onehot
    slot_ids = jnp.sum(earlier * onehot, axis=1)
    places = flat_ids * capacity + slot_ids
    empty = jnp.full((expert_total * capacity,), pair_count, jnp.int32)
    pair_of = empty.at[places].set(jnp.arange(pair_count, dtype=jnp.int32))
    return (places, pair_of)


def by_rows(latent_in, routes, gates, up_weight, down_weight, out_grad):
    owner_count = lax.axis_size("expert")
    local_experts = up_weight.shape[0]
    expert_total = local_experts * owner_count
    token_rows, route_count = routes.shape
    latent = latent_in.shape[1]
    capacity = 9 * token_rows * route_count // (8 * expert_total)
    places, pair_of = slot_places(routes, expert_total, capacity)
    token_of = pair_of // route_count
    zero_row = jnp.zeros((1, latent), jnp.bfloat16)
    padded_in = jnp.concatenate([latent_in, zero_row], axis=0)
    padded_grad = jnp.concatenate([out_grad, zero_row], axis=0)
    padded_gates = jnp.concatenate([gates.reshape(-1), jnp.zeros((1,), jnp.float32)])
    slot_gates = padded_gates[pair_of]
    send_shape = (owner_count, local_experts * capacity, latent)
    block_shape = (owner_count, local_experts, capacity, latent)
    send_rows = padded_in[token_of].reshape(send_shape)
    send_grad = (
        (slot_gates[:, None] * padded_grad[token_of].astype(jnp.float32))
        .astype(jnp.bfloat16)
        .reshape(send_shape)
    )
    up_full, down_full = (
        lax.all_gather(up_weight, "dp", axis=1, tiled=True),
        lax.all_gather(down_weight, "dp", axis=1, tiled=True),
    )
    arrived = lax.all_to_all(send_rows, "expert", split_axis=0, concat_axis=0, tiled=True)
    forward_rows_four = arrived.reshape(block_shape)
    pre_act = jnp.einsum(
        "secl,elh->sech", forward_rows_four, up_full, preferred_element_type=jnp.float32
    )
    active = jnp.maximum(pre_act, 0.0)
    forward_hidden = (active * active).astype(jnp.bfloat16)
    result = jnp.einsum(
        "sech,ehl->secl", forward_hidden, down_full, preferred_element_type=jnp.float32
    ).astype(jnp.bfloat16)
    rows_four, active, hidden, result = (
        forward_rows_four,
        active,
        forward_hidden,
        result.reshape(send_shape),
    )
    returned = lax.all_to_all(result, "expert", split_axis=0, concat_axis=0, tiled=True)
    arrived_grad = lax.all_to_all(send_grad, "expert", split_axis=0, concat_axis=0, tiled=True)
    backward_grad_four = arrived_grad.reshape(block_shape)
    hidden_grad = jnp.einsum(
        "secl,ehl->sech", backward_grad_four, down_full, preferred_element_type=jnp.float32
    )
    backward_pre_grad = (hidden_grad * 2.0 * active).astype(jnp.bfloat16)
    row_grad = jnp.einsum(
        "sech,elh->secl", backward_pre_grad, up_full, preferred_element_type=jnp.float32
    ).astype(jnp.bfloat16)
    grad_four, pre_grad, row_grad = (
        backward_grad_four,
        backward_pre_grad,
        row_grad.reshape(send_shape),
    )
    returned_grad = lax.all_to_all(row_grad, "expert", split_axis=0, concat_axis=0, tiled=True)
    picked = (
        returned.reshape(expert_total * capacity, latent)[places]
        .reshape(token_rows, route_count, latent)
        .astype(jnp.float32)
    )
    latent_out = jnp.sum(gates[:, :, None] * picked, axis=1).astype(jnp.bfloat16)
    gate_grad = jnp.sum(out_grad.astype(jnp.float32)[:, None, :] * picked, axis=2)
    picked_grad = (
        returned_grad.reshape(expert_total * capacity, latent)[places]
        .reshape(token_rows, route_count, latent)
        .astype(jnp.float32)
    )
    grad_in = jnp.sum(picked_grad, axis=1).astype(jnp.bfloat16)
    up_sum = lax.psum_scatter(
        jnp.einsum(
            "secl,sech->leh", rows_four, pre_grad, preferred_element_type=jnp.float32
        ).astype(jnp.bfloat16),
        "dp",
        scatter_dimension=0,
        tiled=True,
    ).astype(jnp.float32)
    down_sum = lax.psum_scatter(
        jnp.einsum("sech,secl->hel", hidden, grad_four, preferred_element_type=jnp.float32).astype(
            jnp.bfloat16
        ),
        "dp",
        scatter_dimension=0,
        tiled=True,
    ).astype(jnp.float32)
    grad_up = jnp.transpose(up_sum, (1, 0, 2))
    grad_down = jnp.transpose(down_sum, (1, 0, 2))
    return (latent_out, grad_in, gate_grad, grad_up, grad_down)


def local(*args):
    owners, parts = lax.axis_size("expert"), lax.axis_size("dp")
    block, latent = args[0].shape
    experts, depth, hid = args[3].shape
    square = parts == 4 and lax.axis_size("group") == 2 and hid == latent and depth * 4 == hid and hid % 512 == 0
    small = block * owners * parts <= 1024 and latent <= 1024 and experts * owners <= LANES
    if square and small and experts == 4 and owners > 1 and block % 16 == 0:
        return by_tokens(*args)
    return by_rows(*args)


def solution(mesh):
    tokens = P(("group", "expert", "dp"), None)
    weights = P("expert", "dp", None)
    grads = P(("group", "expert"), "dp", None)
    return jax.shard_map(
        local,
        mesh=mesh,
        in_specs=(tokens, tokens, tokens, weights, weights, tokens),
        out_specs=(tokens, tokens, tokens, grads, grads),
        check_vma=False,
    )
```
